32 devices in a mesh: wide: 8 (over z, x), narrow: 4 (over y, core).
Axes of the slice: x: 2, y: 2, z: 4, core: 2. Of those that a mesh axis runs over, the one named last changes fastest.
Arguments:
- jacobian: bfloat16 [2048, 16384], P(None, ('wide', 'narrow')), may hold values from -0.125 to 0.125
- variance: float32 [2048], replicated, may hold values from 0.1 to 10
Outputs:
- hessian: float32 [16384, 16384], P('wide', 'narrow')
The draws below stay inside these ranges and needn't reach their ends.
All inputs are finite; a program needn't handle non-finite values.
Results may differ from the reference program's by a relative error of at most 0.004.
Values may be sent and summed in bfloat16 or wider, within the bound.
No kernel may reach another device: no remote copies, remote signals or barrier semaphores. Data moves between devices by JAX's collectives and lax.ppermute only.
A program may use at most 128 MiB of HBM per device.

```python
import math
import jax
import jax.numpy as jnp
from jax import lax

STATE = 16384
OBS = 2048


def block_scale(own_key, extent, pieces, smallest, largest):
    def one(axis_at, shards_of):
        draws = jax.random.uniform(jax.random.fold_in(jax.random.fold_in(own_key, 6), axis_at), (shards_of,), jnp.float32, smallest / len(pieces), largest / len(pieces))
        return jnp.repeat(jnp.exp(draws), extent[axis_at] // shards_of).reshape((-1,) + (1,) * (len(extent) - axis_at - 1))

    gain = one(*pieces[0])
    for cut in pieces[1:]:
        gain = gain * one(*cut)
    return gain


def centred(stream_key, shape, width, most, shards=(), dtype=jnp.bfloat16):
    result = width * jax.random.normal(stream_key, shape, jnp.float32)
    if shards:
        result = result * block_scale(stream_key, shape, shards, -0.22, 0.18)
    return jnp.clip(result, -most, most).astype(dtype)


def setup_inputs(seed: int = 0) -> dict:
    keys = jax.random.split(jax.random.key(seed), 3)
    jacobian = centred(keys[0], (OBS, STATE), OBS ** -0.5, 0.125, ((1, 32),))
    variance = jnp.clip(jnp.exp(jax.random.uniform(keys[1], (OBS,), jnp.float32, math.log(0.1), math.log(10.0))), 0.1, 10.0)
    return {"jacobian": jacobian, "variance": variance}


def reference(jacobian, variance):
    weights = lax.rsqrt(variance)
    scaled = (jacobian.astype(jnp.float32) * weights[:, None]).astype(jnp.bfloat16)
    return lax.dot_general(scaled, scaled, (((0,), (0,)), ((), ())), preferred_element_type=jnp.float32)
```

```python
import jax
import jax.numpy as jnp
from jax import lax
from jax.sharding import PartitionSpec as P

AXES = ("wide", "narrow")
CORES = 2
LANES = 128


class Layout:
    def __init__(self, mesh):
        self.wide, self.narrow = mesh.shape["wide"], mesh.shape["narrow"]
        self.xs = self.wide // self.narrow
        self.zs = self.narrow
        self.ys = self.narrow // CORES
        self.sites = [
            (z, x, y, c)
            for z in range(self.zs)
            for x in range(self.xs)
            for y in range(self.ys)
            for c in range(CORES)
        ]

    def index(self, z, x, y, c):
        return ((z * self.xs + x) * self.ys + y) * CORES + c

    def moves(self, target):
        pairs = []
        for site in self.sites:
            to = target(*site)
            if to is not None:
                pairs.append((self.index(*site), self.index(*to)))
        return pairs


def weigh(panel, row_scale):
    return (panel.astype(jnp.float32) * row_scale).astype(jnp.bfloat16)


def natural(z, c):
    return c == z % CORES


def inner(z):
    return (z % 4 == 1) | (z % 4 == 2)


def choose(options, index):
    picked = options[0]
    for at in range(1, len(options)):
        picked = jnp.where(index == at, options[at], picked)
    return picked


def solution(mesh):
    lay = Layout(mesh)

    def send(value, target):
        return lax.ppermute(value, AXES, lay.moves(target))

    def body(jacobian, variance):
        depth, width = jacobian.shape
        parts = max(width // LANES, 1)
        step = width // parts
        wide_at, narrow_at = lax.axis_index("wide"), lax.axis_index("narrow")
        z, x = wide_at // lay.xs, wide_at % lay.xs
        y, c = narrow_at // CORES, narrow_at % CORES
        half = z // CORES

        row_scale = lax.rsqrt(variance)[:, None]
        own = [weigh(jacobian[:, j * step : (j + 1) * step], row_scale) for j in range(parts)]
        mate = [send(o, lambda z, x, y, c: (z, x, y, 1 - c)) for o in own]
        row_parts = {(0, 0): own, (0, 1): mate}
        for m in range(1, lay.ys):
            row_parts[m, 0] = [send(o, lambda z, x, y, c: (z, x, y ^ m, c)) for o in own]
            row_parts[m, 1] = [
                send(o, lambda z, x, y, c: (z, x, y, 1 - c)) for o in row_parts[m, 0]
            ]

        columns = {}
        for j in range(parts):
            for side in range(2):
                chunk = (own, mate)[side][j]
                paired = send(chunk, lambda z, x, y, c: (z ^ 1, x, y, c) if natural(z, c) else None)
                near = jnp.where(natural(z, c), chunk, paired)
                items = [near]
                if lay.zs > CORES:
                    crossed = send(near, lambda z, x, y, c: (z ^ 3, x, y, c) if inner(z) else None)
                    passed = send(crossed, lambda z, x, y, c: (z ^ 1, x, y, c) if inner(z) else None)
                    items.append(jnp.where(inner(z), crossed, passed))
                for q in range(2, lay.zs // CORES):
                    items.append(send(near, lambda z, x, y, c: (z ^ (CORES * q), x, y, c)))
                for m in range(lay.ys):
                    picked = choose(items, half ^ y ^ m)
                    if m:
                        picked = send(picked, lambda z, x, y, c: (z, x, y ^ m, c))
                    columns[0, m, side, j] = picked
                    for s in range(1, lay.xs):
                        columns[s, m, side, j] = send(
                            picked, lambda z, x, y, c: (z, (x + s) % lay.xs, y, c)
                        )

        rows = jnp.zeros((depth, lay.narrow * width), jnp.bfloat16)
        for (m, side), pieces in row_parts.items():
            at = ((y ^ m) * CORES + (c ^ side)) * width
            rows = lax.dynamic_update_slice(rows, jnp.concatenate(pieces, axis=1), (0, at))

        tile = jnp.zeros((lay.narrow * width, lay.xs * lay.narrow * width), jnp.float32)
        for (s, m, side, j), chunk in columns.items():
            product = lax.dot_general(
                rows, chunk, (((0,), (0,)), ((), ())), preferred_element_type=jnp.float32
            )
            block = ((x - s) % lay.xs * lay.ys + (y ^ m)) * CORES + (c ^ side)
            tile = lax.dynamic_update_slice(tile, product, (0, block * width + j * step))
        return tile

    placed = (P(None, AXES), P())
    return jax.shard_map(
        body, mesh=mesh, in_specs=placed, out_specs=P("wide", "narrow"), check_vma=False
    )
```

```python
import jax
import jax.numpy as jnp
from jax import lax
from jax.experimental import pallas as pl
from jax.experimental.pallas import tpu as pltpu
from jax.sharding import PartitionSpec as P

AXES = ("wide", "narrow")
CORES = 2
LANES = 128
PARTS = 2
TURN = 512
VMEM_MIB = 24


class Layout:
    def __init__(self, mesh):
        self.wide, self.narrow = mesh.shape["wide"], mesh.shape["narrow"]
        self.xs = self.wide // self.narrow
        self.zs = self.narrow
        self.ys = self.narrow // CORES
        self.sites = [
            (z, x, y, c)
            for z in range(self.zs)
            for x in range(self.xs)
            for y in range(self.ys)
            for c in range(CORES)
        ]

    def index(self, z, x, y, c):
        return ((z * self.xs + x) * self.ys + y) * CORES + c

    def moves(self, target):
        pairs = []
        for site in self.sites:
            to = target(*site)
            if to is not None:
                pairs.append((self.index(*site), self.index(*to)))
        return pairs


def weigh(panel, row_scale):
    return (panel.astype(jnp.float32) * row_scale).astype(jnp.bfloat16)


def inner(z):
    return (z % 4 == 1) | (z % 4 == 2)


def apart(z, y):
    return (z // CORES) ^ y


def choose(options, index):
    picked = options[0]
    for at in range(1, len(options)):
        picked = jnp.where(index == at, options[at], picked)
    return picked


def to_mate(z, x, y, c):
    return z, x, y, 1 - c


def to_pair(z, x, y, c):
    return z ^ 1, x, y, c


def to_cross(z, x, y, c):
    return (z ^ 3, x, y, c) if inner(z) else None


def to_outer(z, x, y, c):
    return (z ^ 1, x, y, c) if inner(z) else None


def to_back(z, x, y, c):
    return (z, x, y ^ 1, c) if apart(z, y) == 0 else None


def to_far(q):
    return lambda z, x, y, c: (z ^ (CORES * q), x, y, c)


def along_y(m):
    return lambda z, x, y, c: (z, x, y ^ m, c)


def along_x(lay, s, who=lambda z, y: True):
    return lambda z, x, y, c: (z, (x + s) % lay.xs, y, c) if who(z, y) else None


def turn(rows, chunks, at, shape):
    depth, step = chunks[0].shape

    def kernel(*refs):
        chunk_refs, out_ref, token_ref = refs[: len(chunks)], refs[-2], refs[-1]
        for k, ref in enumerate(chunk_refs):
            out_ref[k * step : (k + 1) * step, :] = ref[...].T
        token_ref[...] = jnp.zeros_like(token_ref)

    operands = list(chunks)
    in_specs = [pl.BlockSpec((TURN, step), lambda i: (i, 0)) for _ in chunks]
    aliases = {}
    if rows is not None:
        operands.append(rows)
        in_specs.append(pl.BlockSpec(memory_space=pl.ANY))
        aliases = {len(operands) - 1: 0}
    return pl.pallas_call(
        kernel,
        grid=(depth // TURN,),
        in_specs=in_specs,
        out_specs=[
            pl.BlockSpec((step * len(chunks), TURN), lambda i: (at, i)),
            pl.BlockSpec((8, LANES), lambda i: (0, 0)),
        ],
        out_shape=[
            jax.ShapeDtypeStruct(shape, jnp.bfloat16),
            jax.ShapeDtypeStruct((8, LANES), jnp.float32),
        ],
        input_output_aliases=aliases,
        compiler_params=pltpu.CompilerParams(vmem_limit_bytes=VMEM_MIB * 2**20),
        cost_estimate=pl.CostEstimate(
            flops=0, bytes_accessed=4 * depth * step * len(chunks), transcendentals=0
        ),
    )(*operands)


def multiply(tile, rows, chunks, blocks, place, shape, band):
    high, depth = rows.shape
    step, count = chunks[0].shape[1], len(chunks)
    bands = high // band

    def kernel(blocks_ref, place_ref, rows_ref, *refs):
        chunk_refs = refs[:count]
        tile_ref, token_ref, result, sems = refs[-4:]
        i = pl.program_id(0)

        def copies(i):
            at = pl.multiple_of((i ^ place_ref[0]) * band, band)
            return [
                pltpu.make_async_copy(
                    result.at[i % 2, :, k * step : (k + 1) * step],
                    tile_ref.at[pl.ds(at, band), pl.ds(pl.multiple_of(blocks_ref[k] * step, step), step)],
                    sems.at[i % 2, k],
                )
                for k in range(count)
            ]

        @pl.when(i >= 2)
        def _():
            for copy in copies(i - 2):
                copy.wait()

        right = jnp.concatenate([ref[...] for ref in chunk_refs], axis=1)
        result[i % 2] = jnp.dot(rows_ref[...], right, preferred_element_type=jnp.float32)
        for copy in copies(i):
            copy.start()

        @pl.when(i == bands - 1)
        def _():
            token_ref[...] = jnp.zeros_like(token_ref)
            for last in range(max(bands - 2, 0), bands):
                for copy in copies(last):
                    copy.wait()

    operands = [rows, *chunks]
    in_specs = [pl.BlockSpec((band, depth), lambda i, b, p: (i, 0))]
    in_specs += [pl.BlockSpec((depth, step), lambda i, b, p: (0, 0)) for _ in chunks]
    aliases = {}
    if tile is not None:
        operands.append(tile)
        in_specs.append(pl.BlockSpec(memory_space=pl.ANY))
        aliases = {len(operands) + 1: 0}
    return pl.pallas_call(
        kernel,
        grid_spec=pltpu.PrefetchScalarGridSpec(
            num_scalar_prefetch=2,
            grid=(bands,),
            in_specs=in_specs,
            out_specs=[
                pl.BlockSpec(memory_space=pl.ANY),
                pl.BlockSpec((8, LANES), lambda i, b, p: (0, 0)),
            ],
            scratch_shapes=[
                pltpu.VMEM((2, band, step * count), jnp.float32),
                pltpu.SemaphoreType.DMA((2, count)),
            ],
        ),
        out_shape=[
            jax.ShapeDtypeStruct(shape, jnp.float32),
            jax.ShapeDtypeStruct((8, LANES), jnp.float32),
        ],
        input_output_aliases=aliases,
        compiler_params=pltpu.CompilerParams(vmem_limit_bytes=VMEM_MIB * 2**20),
        cost_estimate=pl.CostEstimate(
            flops=2 * high * depth * step * count,
            bytes_accessed=2 * high * depth + (2 * depth + 4 * high) * step * count,
            transcendentals=0,
        ),
    )(jnp.stack(blocks), place[None], *operands)


def solution(mesh):
    lay = Layout(mesh)

    def body(jacobian, variance):
        depth, width = jacobian.shape
        step = width // PARTS
        shape = (lay.narrow * width, lay.xs * lay.narrow * width)
        wide_at, narrow_at = lax.axis_index("wide"), lax.axis_index("narrow")
        z, x = wide_at // lay.xs, wide_at % lay.xs
        y, c = narrow_at // CORES, narrow_at % CORES
        is_inner, off = inner(z), apart(z, y)
        home, beside = off == 0, off == 1
        halves, others, shifts = range(2, lay.zs // CORES), range(1, lay.ys), range(1, lay.xs)
        first_kept = ((z % CORES) ^ (is_inner & beside)) == c

        row_scale = lax.rsqrt(variance)[:, None]
        got = {}
        for h in range(PARTS):
            got["own", h] = weigh(jacobian[:, h * step : (h + 1) * step], row_scale)
        running = []

        def across(kind, h):
            return jnp.where(is_inner, got[kind + "_cross", h], got[kind + "_outer", h])

        def first(h, q):
            options = [got["own", h], across("own", h)] + [got["far_own", h, n] for n in halves]
            return choose(options, q)

        def second(h, q):
            options = [got["pair", h], across("pair", h)] + [got["far_pair", h, n] for n in halves]
            return choose(options, q)

        def send(name, value, target):
            running.append((name, lax.ppermute(value, AXES, lay.moves(target))))

        def settle(barrier=True):
            got.update(running)
            running.clear()
            if barrier:
                got.update(zip(got, lax.optimization_barrier(tuple(got.values()))))


        def pair(h):
            send(("pair", h), got["own", h], to_pair)

        def cross(kind, h):
            send((kind + "_cross", h), got[kind, h], to_cross)
            for n in halves:
                send(("far_" + kind, h, n), got[kind, h], to_far(n))

        def outer(kind, h):
            send((kind + "_outer", h), got[kind + "_cross", h], to_outer)


        def row(h):
            for m in others:
                send(("row", h, m), got["own", h], along_y(m))

        def give(h):
            for m in others:
                value = jnp.where(off == m, got["pair", h], first(h, off ^ m))
                send(("give", h, m), value, along_y(m))

        def give_more(h):
            for m in others:
                value = jnp.where(off == m, got["own_x", h, 1], second(h, off ^ m))
                send(("give_more", h, m), value, along_y(m))

        def own_x(h):
            for s in shifts:
                send(("own_x", h, s), got["own", h], along_x(lay, s))

        def near_x(h):
            value = jnp.where(home, got["pair", h], first(h, off))
            for s in shifts:
                send(("near_x", h, s), value, along_x(lay, s))

        def more_x(h):
            for m in others:
                value = jnp.where(home, got["give", h, m], second(h, off))
                for s in shifts:
                    who = lambda z, y, m=m: m == 1 or apart(z, y) == 0
                    send(("more_x", h, s, m), value, along_x(lay, s, who))
                    rest = lambda z, y, m=m: apart(z, y) > 1 or (apart(z, y) == 1 and m != 1)
                    if lay.ys > 2:
                        send(("rest_x", h, s, m), got["give_more", h, m], along_x(lay, s, rest))

        def give_x(h):
            for m in others:
                value = jnp.where(home, second(h, 1), got["give", h, m])
                for s in shifts:
                    who = lambda z, y, m=m: m == 1 or apart(z, y) != 0
                    send(("give_x", h, s, m), value, along_x(lay, s, who))

        def back(h):
            for s in shifts:
                send(("back", h, s), got["give_x", h, s, 1], to_back)


        def mate(kind, h):
            for name in [n for n in got if n[0] == kind and n[1] == h]:
                send((kind + "_mate", *name[1:]), got[name], to_mate)

        def places(kind):
            return [(s, m) for s in (shifts if "x" in kind else (0,)) for m in (others if "y" in kind else (0,))]

        def both(h, s, m):
            if s == 0 and m == 0:
                return first(h, off), second(h, off)
            if s == 0:
                return (
                    jnp.where(home, got["row", h, m], got["give", h, m]),
                    jnp.where(home, got["give", h, m], got["give_more", h, m]),
                )
            if m == 0:
                return (
                    jnp.where(home, got["own_x", h, s], got["near_x", h, s]),
                    jnp.where(home, got["near_x", h, s], got["more_x", h, s, 1]),
                )
            last = got.get(("rest_x", h, s, m), got["back", h, s])
            if m == 1 and lay.ys > 2:
                last = jnp.where(beside, got["back", h, s], last)
            return (
                jnp.where(home, got["give_more", h, m], got["give_x", h, s, m]),
                jnp.where(home, got["more_x", h, s, m], last),
            )

        def swap(kind, h):
            for s, m in places(kind):
                one, two = both(h, s, m)
                got["kept", h, s, m] = jnp.where(first_kept, one, two)
                send(("swapped", h, s, m), jnp.where(first_kept, two, one), to_mate)


        def lay_row(m, side):
            kind = ("row" if m else "own") + ("_mate" if side else "")
            chunks = [got[(kind, h, m) if m else (kind, h)] for h in range(PARTS)]
            band = m * CORES + side
            if step % LANES:
                rows = got.get("rows")
                rows = jnp.zeros((depth, shape[0]), jnp.bfloat16) if rows is None else rows
                value = jnp.concatenate(chunks, axis=1)
                got["rows"] = lax.dynamic_update_slice(rows, value, (0, (narrow_at ^ band) * width))
            else:
                got["rows"], got["mark", "row", band] = turn(got.get("rows"), chunks, band, (shape[0], depth))

        def product(h, *kinds, sides=(0, 1)):
            chunks, blocks = [], []
            for kind in kinds:
                for s, m in places(kind):
                    for side in sides:
                        chunks.append(got["swapped" if side else "kept", h, s, m])
                        block = ((x - s) % lay.xs * lay.ys + (y ^ m)) * CORES + (c ^ side)
                        blocks.append(block * PARTS + h)
            tile = got.get("tile")
            if step % LANES:
                tile = jnp.zeros(shape, jnp.float32) if tile is None else tile
                for chunk, block in zip(chunks, blocks):
                    dims = (((0,), (0,)), ((), ()))
                    part = lax.dot_general(got["rows"], chunk, dims, preferred_element_type=jnp.float32)
                    tile = lax.dynamic_update_slice(tile, part, (0, block * step))
                got["tile"] = tile
            else:
                got["tile"], got["mark", "tile"] = multiply(tile, got["rows"], chunks, blocks, narrow_at, shape, width)

        pair(0)
        cross("own", 0)
        own_x(0)
        row(0)
        mate("own", 0)
        settle()

        outer("own", 0)
        cross("pair", 0)
        own_x(1)
        row(1)
        mate("own", 1)
        settle()

        outer("pair", 0)
        cross("own", 1)
        near_x(0)
        give(0)
        mate("row", 0)
        lay_row(0, 0)
        settle()

        pair(1)
        give_x(0)
        give_more(0)
        mate("row", 1)
        swap("", 0)
        lay_row(0, 1)
        settle()

        outer("own", 1)
        cross("pair", 1)
        more_x(0)
        back(0)
        swap("y", 0)
        for m in others:
            lay_row(m, 0)
            lay_row(m, 1)
        settle()

        outer("pair", 1)
        near_x(1)
        give(1)
        swap("x", 0)
        swap("xy", 0)
        product(0, "", "y")
        settle()

        give_x(1)
        give_more(1)
        swap("", 1)
        product(0, "x", "xy")
        settle()

        more_x(1)
        back(1)
        swap("y", 1)
        product(1, "")
        settle()

        swap("x", 1)
        swap("xy", 1)
        product(1, "y")
        product(1, "x", "xy", sides=(0,))
        settle()

        product(1, "x", "xy", sides=(1,))
        return got["tile"]

    placed = (P(None, AXES), P())
    return jax.shard_map(
        body, mesh=mesh, in_specs=placed, out_specs=P("wide", "narrow"), check_vma=False
    )
```

```python
import jax
import jax.numpy as jnp
from jax import lax
from jax.experimental import pallas as pl
from jax.experimental.pallas import tpu as pltpu
from jax.sharding import PartitionSpec as P

AXES = ("wide", "narrow")
CORES = 2
LANES = 128
PARTS = 2
TURN = 512
VMEM_MIB = 24


class Layout:
    def __init__(self, mesh):
        self.wide, self.narrow = mesh.shape["wide"], mesh.shape["narrow"]
        self.xs = self.wide // self.narrow
        self.zs = self.narrow
        self.ys = self.narrow // CORES
        self.sites = [
            (z, x, y, c)
            for z in range(self.zs)
            for x in range(self.xs)
            for y in range(self.ys)
            for c in range(CORES)
        ]

    def index(self, z, x, y, c):
        return ((z * self.xs + x) * self.ys + y) * CORES + c

    def moves(self, target):
        pairs = []
        for site in self.sites:
            to = target(*site)
            if to is not None:
                pairs.append((self.index(*site), self.index(*to)))
        return pairs


def weigh(panel, row_scale):
    return (panel.astype(jnp.float32) * row_scale).astype(jnp.bfloat16)


def inner(z):
    return (z % 4 == 1) | (z % 4 == 2)


def apart(z, y):
    return (z // CORES) ^ y


def choose(options, index):
    picked = options[0]
    for at in range(1, len(options)):
        picked = jnp.where(index == at, options[at], picked)
    return picked


def to_mate(z, x, y, c):
    return z, x, y, 1 - c


def to_pair(z, x, y, c):
    return z ^ 1, x, y, c


def to_cross(z, x, y, c):
    return (z ^ 3, x, y, c) if inner(z) else None


def to_outer(z, x, y, c):
    return (z ^ 1, x, y, c) if inner(z) else None


def to_far(q):
    return lambda z, x, y, c: (z ^ (CORES * q), x, y, c)


def along_y(m):
    return lambda z, x, y, c: (z, x, y ^ m, c)


def along_x(lay, s, who=lambda z, y: True):
    return lambda z, x, y, c: (z, (x + s) % lay.xs, y, c) if who(z, y) else None


def turn(rows, chunks, at, shape):
    depth, step = chunks[0].shape

    def kernel(*refs):
        chunk_refs, out_ref, token_ref = refs[: len(chunks)], refs[-2], refs[-1]
        for k, ref in enumerate(chunk_refs):
            out_ref[k * step : (k + 1) * step, :] = ref[...].T
        token_ref[...] = jnp.zeros_like(token_ref)

    operands = list(chunks)
    in_specs = [pl.BlockSpec((TURN, step), lambda i: (i, 0)) for _ in chunks]
    aliases = {}
    if rows is not None:
        operands.append(rows)
        in_specs.append(pl.BlockSpec(memory_space=pl.ANY))
        aliases = {len(operands) - 1: 0}
    return pl.pallas_call(
        kernel,
        grid=(depth // TURN,),
        in_specs=in_specs,
        out_specs=[
            pl.BlockSpec((step * len(chunks), TURN), lambda i: (at, i)),
            pl.BlockSpec((8, LANES), lambda i: (0, 0)),
        ],
        out_shape=[
            jax.ShapeDtypeStruct(shape, jnp.bfloat16),
            jax.ShapeDtypeStruct((8, LANES), jnp.float32),
        ],
        input_output_aliases=aliases,
        compiler_params=pltpu.CompilerParams(vmem_limit_bytes=VMEM_MIB * 2**20),
        cost_estimate=pl.CostEstimate(
            flops=0, bytes_accessed=4 * depth * step * len(chunks), transcendentals=0
        ),
    )(*operands)


def multiply(tile, rows, columns, blocks, place, shape, band):
    high, depth = rows.shape
    step, count = columns[0][0][0].shape[1], len(columns)
    bands = high // band
    options = [arrays for arrays, _ in columns]
    picks = [jnp.asarray(pick, jnp.int32) for _, pick in columns]
    flat = sum(options, [])

    def kernel(blocks_ref, place_ref, picks_ref, rows_ref, *refs):
        tile_ref, token_ref, right, result, in_sems, out_sems = refs[-6:]
        i = pl.program_id(0)

        def fetch(act):
            at = 0
            for k, arrays in enumerate(options):
                for n in range(len(arrays)):

                    @pl.when(picks_ref[k] == n)
                    def _(k=k, source=refs[at + n]):
                        act(pltpu.make_async_copy(source, right.at[:, k * step : (k + 1) * step], in_sems.at[k]))

                at += len(arrays)

        def copies(i):
            at = pl.multiple_of((i ^ place_ref[0]) * band, band)
            return [
                pltpu.make_async_copy(
                    result.at[i % 2, :, k * step : (k + 1) * step],
                    tile_ref.at[pl.ds(at, band), pl.ds(pl.multiple_of(blocks_ref[k] * step, step), step)],
                    out_sems.at[i % 2, k],
                )
                for k in range(count)
            ]

        @pl.when(i == 0)
        def _():
            fetch(lambda copy: copy.start())
            fetch(lambda copy: copy.wait())

        @pl.when(i >= 2)
        def _():
            for copy in copies(i - 2):
                copy.wait()

        result[i % 2] = jnp.dot(rows_ref[...], right[...], preferred_element_type=jnp.float32)
        for copy in copies(i):
            copy.start()

        @pl.when(i == bands - 1)
        def _():
            token_ref[...] = jnp.zeros_like(token_ref)
            for last in range(max(bands - 2, 0), bands):
                for copy in copies(last):
                    copy.wait()

    operands = [rows, *flat]
    in_specs = [pl.BlockSpec((band, depth), lambda i, b, p, k: (i, 0))]
    in_specs += [pl.BlockSpec(memory_space=pl.ANY) for _ in flat]
    aliases = {}
    if tile is not None:
        operands.append(tile)
        in_specs.append(pl.BlockSpec(memory_space=pl.ANY))
        aliases = {len(operands) + 2: 0}
    return pl.pallas_call(
        kernel,
        grid_spec=pltpu.PrefetchScalarGridSpec(
            num_scalar_prefetch=3,
            grid=(bands,),
            in_specs=in_specs,
            out_specs=[
                pl.BlockSpec(memory_space=pl.ANY),
                pl.BlockSpec((8, LANES), lambda i, b, p, k: (0, 0)),
            ],
            scratch_shapes=[
                pltpu.VMEM((depth, step * count), jnp.bfloat16),
                pltpu.VMEM((2, band, step * count), jnp.float32),
                pltpu.SemaphoreType.DMA((count,)),
                pltpu.SemaphoreType.DMA((2, count)),
            ],
        ),
        out_shape=[
            jax.ShapeDtypeStruct(shape, jnp.float32),
            jax.ShapeDtypeStruct((8, LANES), jnp.float32),
        ],
        input_output_aliases=aliases,
        compiler_params=pltpu.CompilerParams(vmem_limit_bytes=VMEM_MIB * 2**20),
        cost_estimate=pl.CostEstimate(
            flops=2 * high * depth * step * count,
            bytes_accessed=2 * high * depth + (2 * depth + 4 * high) * step * count,
            transcendentals=0,
        ),
    )(jnp.stack(blocks), place[None], jnp.stack(picks), *operands)


def solution(mesh):
    lay = Layout(mesh)

    def body(jacobian, variance):
        depth, width = jacobian.shape
        step = width // PARTS
        shape = (lay.narrow * width, lay.xs * lay.narrow * width)
        wide_at, narrow_at = lax.axis_index("wide"), lax.axis_index("narrow")
        z, x = wide_at // lay.xs, wide_at % lay.xs
        y, c = narrow_at // CORES, narrow_at % CORES
        is_inner, off = inner(z), apart(z, y)
        home, beside = off == 0, off == 1
        halves, others, shifts = range(2, lay.zs // CORES), range(1, lay.ys), range(1, lay.xs)
        first_kept = ((z % CORES) ^ (is_inner & beside)) == c

        row_scale = lax.rsqrt(variance)[:, None]
        got = {}
        for h in range(PARTS):
            got["own", h] = weigh(jacobian[:, h * step : (h + 1) * step], row_scale)
        running = []

        def across(kind, h):
            return jnp.where(is_inner, got[kind + "_cross", h], got[kind + "_outer", h])

        def first(h, q):
            options = [got["own", h], across("own", h)] + [got["far_own", h, n] for n in halves]
            return choose(options, q)

        def second(h, q):
            options = [got["pair", h], across("pair", h)] + [got["far_pair", h, n] for n in halves]
            return choose(options, q)

        def send(name, value, target):
            running.append((name, lax.ppermute(value, AXES, lay.moves(target))))

        def settle(barrier=True):
            got.update(running)
            running.clear()
            if barrier:
                got.update(zip(got, lax.optimization_barrier(tuple(got.values()))))


        def pair(h):
            send(("pair", h), got["own", h], to_pair)

        def cross(kind, h):
            send((kind + "_cross", h), got[kind, h], to_cross)
            for n in halves:
                send(("far_" + kind, h, n), got[kind, h], to_far(n))

        def outer(kind, h):
            send((kind + "_outer", h), got[kind + "_cross", h], to_outer)


        def row(h):
            for m in others:
                send(("row", h, m), got["own", h], along_y(m))

        def row_of(core, h):
            for m in others:
                who = lambda z, x, y, c, m=m: (z, x, y ^ m, c) if c == core else None
                send(("row_of", h, m, core), got["own", h], who)

        def join_rows(h):
            for m in others:
                got["row", h, m] = jnp.where(c == 0, got["row_of", h, m, 0], got["row_of", h, m, 1])

        def give(h):
            for m in others:
                value = jnp.where(off == m, got["pair", h], first(h, off ^ m))
                send(("give", h, m), value, along_y(m))

        def give_more(h):
            for m in others:
                value = jnp.where(off == m, got["own_x", h, 1], second(h, off ^ m))
                send(("give_more", h, m), value, along_y(m))

        def own_x(h):
            for s in shifts:
                send(("own_x", h, s), got["own", h], along_x(lay, s))

        def near_x(h):
            value = jnp.where(home, got["pair", h], first(h, off))
            for s in shifts:
                send(("near_x", h, s), value, along_x(lay, s))

        def more_x(h):
            for m in others:
                value = jnp.where(home, got["give", h, m], second(h, off))
                for s in shifts:
                    who = lambda z, y, m=m: m == 1 or apart(z, y) == 0
                    send(("more_x", h, s, m), value, along_x(lay, s, who))
                    rest = lambda z, y, m=m: apart(z, y) > 1 or (apart(z, y) == 1 and m != 1)
                    if lay.ys > 2:
                        send(("rest_x", h, s, m), got["give_more", h, m], along_x(lay, s, rest))

        def give_x(h):
            for m in others:
                value = jnp.where(home, second(h, 1), got["give", h, m])
                for s in shifts:
                    who = lambda z, y, m=m: m == 1 or apart(z, y) != 0
                    send(("give_x", h, s, m), value, along_x(lay, s, who))

        def back(h):
            for s in shifts:
                send(("back", h, s), got["give_x", h, s, 1], along_y(1))


        def mate(kind, h):
            for name in [n for n in got if n[0] == kind and n[1] == h]:
                send((kind + "_mate", *name[1:]), got[name], to_mate)

        def places(kind):
            return [(s, m) for s in (shifts if "x" in kind else (0,)) for m in (others if "y" in kind else (0,))]

        def both(h, s, m):
            away = jnp.where(home, 0, 1)
            if s == 0 and m == 0:
                which = jnp.where(beside, jnp.where(is_inner, 1, 2), jnp.where(home, 0, off + 1))
                sources = []
                for kind in ("own", "pair"):
                    names = [(kind, h), (kind + "_cross", h), (kind + "_outer", h)]
                    names += [("far_" + kind, h, n) for n in halves]
                    sources.append(([got[n] for n in names], which))
                return sources
            if s == 0:
                return ([got["row", h, m], got["give", h, m]], away), ([got["give", h, m], got["give_more", h, m]], away)
            if m == 0:
                return (
                    ([got["own_x", h, s], got["near_x", h, s]], away),
                    ([got["near_x", h, s], got["more_x", h, s, 1]], away),
                )
            last, which = [got["more_x", h, s, m], got["back", h, s]], away
            if lay.ys > 2:
                last.append(got["rest_x", h, s, m])
                which = jnp.where(home, 0, jnp.where(beside & (m == 1), 1, 2))
            return ([got["give_more", h, m], got["give_x", h, s, m]], away), (last, which)

        def kept(h, s, m):
            (one, which_one), (two, which_two) = both(h, s, m)
            return one + two, jnp.where(first_kept, which_one, len(one) + which_two)

        def swap(kind, h):
            for s, m in places(kind):
                one, two = both(h, s, m)
                send(("swapped", h, s, m), jnp.where(first_kept, choose(*two), choose(*one)), to_mate)


        def lay_row(m, side):
            kind = ("row" if m else "own") + ("_mate" if side else "")
            chunks = [got[(kind, h, m) if m else (kind, h)] for h in range(PARTS)]
            band = m * CORES + side
            if step % LANES:
                rows = got.get("rows")
                rows = jnp.zeros((depth, shape[0]), jnp.bfloat16) if rows is None else rows
                value = jnp.concatenate(chunks, axis=1)
                got["rows"] = lax.dynamic_update_slice(rows, value, (0, (narrow_at ^ band) * width))
            else:
                got["rows"], got["mark", "row", band] = turn(got.get("rows"), chunks, band, (shape[0], depth))

        def product(h, *kinds, sides=(0, 1)):
            chunks, blocks = [], []
            for kind in kinds:
                for s, m in places(kind):
                    for side in sides:
                        chunks.append(([got["swapped", h, s, m]], 0) if side else kept(h, s, m))
                        block = ((x - s) % lay.xs * lay.ys + (y ^ m)) * CORES + (c ^ side)
                        blocks.append(block * PARTS + h)
            tile = got.get("tile")
            if step % LANES:
                tile = jnp.zeros(shape, jnp.float32) if tile is None else tile
                for chunk, block in zip(chunks, blocks):
                    dims = (((0,), (0,)), ((), ()))
                    part = lax.dot_general(got["rows"], choose(*chunk), dims, preferred_element_type=jnp.float32)
                    tile = lax.dynamic_update_slice(tile, part, (0, block * step))
                got["tile"] = tile
            else:
                got["tile"], got["mark", "tile"] = multiply(tile, got["rows"], chunks, blocks, narrow_at, shape, width)

        row_of(1, 0)
        settle()

        pair(0)
        cross("own", 0)
        own_x(0)
        row_of(0, 0)
        mate("own", 0)
        settle()

        outer("own", 0)
        cross("pair", 0)
        own_x(1)
        row(1)
        mate("own", 1)
        settle()

        outer("pair", 0)
        cross("own", 1)
        near_x(0)
        give(0)
        join_rows(0)
        mate("row", 0)
        lay_row(0, 0)
        settle()

        pair(1)
        give_x(0)
        give_more(0)
        mate("row", 1)
        swap("", 0)
        lay_row(0, 1)
        settle()

        outer("own", 1)
        cross("pair", 1)
        more_x(0)
        back(0)
        swap("y", 0)
        for m in others:
            lay_row(m, 0)
            lay_row(m, 1)
        settle()

        outer("pair", 1)
        near_x(1)
        give(1)
        swap("x", 0)
        swap("xy", 0)
        product(0, "", "y")
        settle()

        give_x(1)
        give_more(1)
        swap("", 1)
        product(0, "x", "xy")
        settle()

        more_x(1)
        back(1)
        swap("y", 1)
        product(1, "")
        product(1, "y", sides=(0,))
        settle()

        swap("x", 1)
        swap("xy", 1)
        product(1, "x", "xy", sides=(0,))
        settle()

        product(1, "y", "x", "xy", sides=(1,))
        return got["tile"]

    placed = (P(None, AXES), P())
    return jax.shard_map(
        body, mesh=mesh, in_specs=placed, out_specs=P("wide", "narrow"), check_vma=False
    )
```

```python
import jax
import jax.numpy as jnp
from jax import lax
from jax.experimental import pallas as pl
from jax.experimental.pallas import tpu as pltpu
from jax.sharding import PartitionSpec as P

AXES = ("wide", "narrow")
CORES = 2
LANES = 128
PARTS = 2
TURN = 512
VMEM_MIB = 24


class Layout:
    def __init__(self, mesh):
        self.wide, self.narrow = mesh.shape["wide"], mesh.shape["narrow"]
        self.xs = self.wide // self.narrow
        self.zs = self.narrow
        self.ys = self.narrow // CORES
        self.sites = [
            (z, x, y, c)
            for z in range(self.zs)
            for x in range(self.xs)
            for y in range(self.ys)
            for c in range(CORES)
        ]

    def index(self, z, x, y, c):
        return ((z * self.xs + x) * self.ys + y) * CORES + c

    def moves(self, target):
        pairs = []
        for site in self.sites:
            to = target(*site)
            if to is not None:
                pairs.append((self.index(*site), self.index(*to)))
        return pairs


def weigh(panel, row_scale):
    return (panel.astype(jnp.float32) * row_scale).astype(jnp.bfloat16)


def inner(z):
    return (z % 4 == 1) | (z % 4 == 2)


def apart(z, y):
    return (z // CORES) ^ y


def choose(options, index):
    picked = options[0]
    for at in range(1, len(options)):
        picked = jnp.where(index == at, options[at], picked)
    return picked


def to_mate(z, x, y, c):
    return z, x, y, 1 - c


def to_pair(z, x, y, c):
    return z ^ 1, x, y, c


def to_cross(z, x, y, c):
    return (z ^ 3, x, y, c) if inner(z) else None


def to_outer(z, x, y, c):
    return (z ^ 1, x, y, c) if inner(z) else None


def to_far(q):
    return lambda z, x, y, c: (z ^ (CORES * q), x, y, c)


def along_y(m):
    return lambda z, x, y, c: (z, x, y ^ m, c)


def along_x(lay, s, who=lambda z, y: True):
    return lambda z, x, y, c: (z, (x + s) % lay.xs, y, c) if who(z, y) else None


def turn(rows, chunks, at, shape):
    depth, step = chunks[0].shape

    def kernel(*refs):
        chunk_refs, out_ref, token_ref = refs[: len(chunks)], refs[-2], refs[-1]
        for k, ref in enumerate(chunk_refs):
            out_ref[k * step : (k + 1) * step, :] = ref[...].T
        token_ref[...] = jnp.zeros_like(token_ref)

    operands = list(chunks)
    in_specs = [pl.BlockSpec((TURN, step), lambda i: (i, 0)) for _ in chunks]
    aliases = {}
    if rows is not None:
        operands.append(rows)
        in_specs.append(pl.BlockSpec(memory_space=pl.ANY))
        aliases = {len(operands) - 1: 0}
    return pl.pallas_call(
        kernel,
        grid=(depth // TURN,),
        in_specs=in_specs,
        out_specs=[
            pl.BlockSpec((step * len(chunks), TURN), lambda i: (at, i)),
            pl.BlockSpec((8, LANES), lambda i: (0, 0)),
        ],
        out_shape=[
            jax.ShapeDtypeStruct(shape, jnp.bfloat16),
            jax.ShapeDtypeStruct((8, LANES), jnp.float32),
        ],
        input_output_aliases=aliases,
        compiler_params=pltpu.CompilerParams(vmem_limit_bytes=VMEM_MIB * 2**20),
        cost_estimate=pl.CostEstimate(
            flops=0, bytes_accessed=4 * depth * step * len(chunks), transcendentals=0
        ),
    )(*operands)


def multiply(tile, rows, chunks, blocks, place, shape, band):
    high, depth = rows.shape
    step, count = chunks[0].shape[1], len(chunks)
    bands = high // band

    def kernel(blocks_ref, place_ref, rows_ref, *refs):
        chunk_refs = refs[:count]
        tile_ref, token_ref, result, sems = refs[-4:]
        i = pl.program_id(0)

        def copies(i):
            at = pl.multiple_of((i ^ place_ref[0]) * band, band)
            return [
                pltpu.make_async_copy(
                    result.at[i % 2, :, k * step : (k + 1) * step],
                    tile_ref.at[pl.ds(at, band), pl.ds(pl.multiple_of(blocks_ref[k] * step, step), step)],
                    sems.at[i % 2, k],
                )
                for k in range(count)
            ]

        @pl.when(i >= 2)
        def _():
            for copy in copies(i - 2):
                copy.wait()

        right = jnp.concatenate([ref[...] for ref in chunk_refs], axis=1)
        result[i % 2] = jnp.dot(rows_ref[...], right, preferred_element_type=jnp.float32)
        for copy in copies(i):
            copy.start()

        @pl.when(i == bands - 1)
        def _():
            token_ref[...] = jnp.zeros_like(token_ref)
            for last in range(max(bands - 2, 0), bands):
                for copy in copies(last):
                    copy.wait()

    operands = [rows, *chunks]
    in_specs = [pl.BlockSpec((band, depth), lambda i, b, p: (i, 0))]
    in_specs += [pl.BlockSpec((depth, step), lambda i, b, p: (0, 0)) for _ in chunks]
    aliases = {}
    if tile is not None:
        operands.append(tile)
        in_specs.append(pl.BlockSpec(memory_space=pl.ANY))
        aliases = {len(operands) + 1: 0}
    return pl.pallas_call(
        kernel,
        grid_spec=pltpu.PrefetchScalarGridSpec(
            num_scalar_prefetch=2,
            grid=(bands,),
            in_specs=in_specs,
            out_specs=[
                pl.BlockSpec(memory_space=pl.ANY),
                pl.BlockSpec((8, LANES), lambda i, b, p: (0, 0)),
            ],
            scratch_shapes=[
                pltpu.VMEM((2, band, step * count), jnp.float32),
                pltpu.SemaphoreType.DMA((2, count)),
            ],
        ),
        out_shape=[
            jax.ShapeDtypeStruct(shape, jnp.float32),
            jax.ShapeDtypeStruct((8, LANES), jnp.float32),
        ],
        input_output_aliases=aliases,
        compiler_params=pltpu.CompilerParams(vmem_limit_bytes=VMEM_MIB * 2**20),
        cost_estimate=pl.CostEstimate(
            flops=2 * high * depth * step * count,
            bytes_accessed=2 * high * depth + (2 * depth + 4 * high) * step * count,
            transcendentals=0,
        ),
    )(jnp.stack(blocks), place[None], *operands)


def solution(mesh):
    lay = Layout(mesh)

    def body(jacobian, variance):
        depth, width = jacobian.shape
        step = width // PARTS
        shape = (lay.narrow * width, lay.xs * lay.narrow * width)
        wide_at, narrow_at = lax.axis_index("wide"), lax.axis_index("narrow")
        z, x = wide_at // lay.xs, wide_at % lay.xs
        y, c = narrow_at // CORES, narrow_at % CORES
        is_inner, off = inner(z), apart(z, y)
        home, beside = off == 0, off == 1
        halves, others, shifts = range(2, lay.zs // CORES), range(1, lay.ys), range(1, lay.xs)
        first_kept = ((z % CORES) ^ (is_inner & beside)) == c

        row_scale = lax.rsqrt(variance)[:, None]
        got = {}
        for h in range(PARTS):
            got["own", h] = weigh(jacobian[:, h * step : (h + 1) * step], row_scale)
        running = []

        def across(kind, h):
            return jnp.where(is_inner, got[kind + "_cross", h], got[kind + "_outer", h])

        def first(h, q):
            options = [got["own", h], across("own", h)] + [got["far_own", h, n] for n in halves]
            return choose(options, q)

        def second(h, q):
            options = [got["pair", h], across("pair", h)] + [got["far_pair", h, n] for n in halves]
            return choose(options, q)

        def send(name, value, target):
            running.append((name, lax.ppermute(value, AXES, lay.moves(target))))

        def settle(*under_way):
            got.update(r for r in running if r[0][:2] not in under_way)
            running[:] = [r for r in running if r[0][:2] in under_way]
            got.update(zip(got, lax.optimization_barrier(tuple(got.values()))))

        def take(kind, h, s, many):
            mine = [r for r in running if r[0][:3] == (kind, h, s) and (r[0][3] > 0) == many]
            got.update(mine)
            running[:] = [r for r in running if r[0] not in [n for n, _ in mine]]


        def pair(h):
            send(("pair", h), got["own", h], to_pair)

        def cross(kind, h):
            send((kind + "_cross", h), got[kind, h], to_cross)
            for n in halves:
                send(("far_" + kind, h, n), got[kind, h], to_far(n))

        def outer(kind, h):
            send((kind + "_outer", h), got[kind + "_cross", h], to_outer)


        def row(h):
            for m in others:
                send(("row", h, m), got["own", h], along_y(m))

        def row_of(core, h):
            for m in others:
                who = lambda z, x, y, c, m=m: (z, x, y ^ m, c) if c == core else None
                send(("row_of", h, m, core), got["own", h], who)

        def join_rows(h):
            for m in others:
                got["row", h, m] = jnp.where(c == 0, got["row_of", h, m, 0], got["row_of", h, m, 1])

        def give(h):
            for m in others:
                value = jnp.where(off == m, got["pair", h], first(h, off ^ m))
                send(("give", h, m), value, along_y(m))

        def give_more(h):
            for m in others:
                value = jnp.where(off == m, got["own_x", h, 1], second(h, off ^ m))
                send(("give_more", h, m), value, along_y(m))

        def own_x(h):
            for s in shifts:
                send(("own_x", h, s), got["own", h], along_x(lay, s))

        def near_x(h):
            value = jnp.where(home, got["pair", h], first(h, off))
            for s in shifts:
                send(("near_x", h, s), value, along_x(lay, s))

        def more_x(h):
            for m in others:
                value = jnp.where(home, got["give", h, m], second(h, off))
                for s in shifts:
                    who = lambda z, y, m=m: m == 1 or apart(z, y) == 0
                    send(("more_x", h, s, m), value, along_x(lay, s, who))
                    rest = lambda z, y, m=m: apart(z, y) > 1 or (apart(z, y) == 1 and m != 1)
                    if lay.ys > 2:
                        send(("rest_x", h, s, m), got["give_more", h, m], along_x(lay, s, rest))

        def give_x(h):
            for m in others:
                value = jnp.where(home, second(h, 1), got["give", h, m])
                for s in shifts:
                    who = lambda z, y, m=m: m == 1 or apart(z, y) != 0
                    send(("give_x", h, s, m), value, along_x(lay, s, who))

        def back(h):
            for s in shifts:
                send(("back", h, s), got["give_x", h, s, 1], along_y(1))


        def mate(kind, h):
            for name in [n for n in got if n[0] == kind and n[1] == h]:
                send((kind + "_mate", *name[1:]), got[name], to_mate)

        def places(kind):
            return [(s, m) for s in (shifts if "x" in kind else (0,)) for m in (others if "y" in kind else (0,))]

        def both(h, s, m):
            if s == 0 and m == 0:
                return first(h, off), second(h, off)
            if s == 0:
                return (
                    jnp.where(home, got["row", h, m], got["give", h, m]),
                    jnp.where(home, got["give", h, m], got["give_more", h, m]),
                )
            if m == 0:
                return (
                    jnp.where(home, got["own_x", h, s], got["near_x", h, s]),
                    jnp.where(home, got["near_x", h, s], got["more_x", h, s, 1]),
                )
            last = got.get(("rest_x", h, s, m), got["back", h, s])
            if m == 1 and lay.ys > 2:
                last = jnp.where(beside, got["back", h, s], last)
            return (
                jnp.where(home, got["give_more", h, m], got["give_x", h, s, m]),
                jnp.where(home, got["more_x", h, s, m], last),
            )

        def swap(kind, h):
            for s, m in places(kind):
                one, two = both(h, s, m)
                got["kept", h, s, m] = jnp.where(first_kept, one, two)
                send(("swapped", h, s, m), jnp.where(first_kept, two, one), to_mate)


        def lay_row(m, side):
            kind = ("row" if m else "own") + ("_mate" if side else "")
            chunks = [got[(kind, h, m) if m else (kind, h)] for h in range(PARTS)]
            band = m * CORES + side
            if step % LANES:
                rows = got.get("rows")
                rows = jnp.zeros((depth, shape[0]), jnp.bfloat16) if rows is None else rows
                value = jnp.concatenate(chunks, axis=1)
                got["rows"] = lax.dynamic_update_slice(rows, value, (0, (narrow_at ^ band) * width))
            else:
                got["rows"], got["mark", "row", band] = turn(got.get("rows"), chunks, band, (shape[0], depth))

        def product(h, *kinds, sides=(0, 1)):
            chunks, blocks = [], []
            for kind in kinds:
                for s, m in places(kind):
                    for side in sides:
                        chunks.append(got["swapped" if side else "kept", h, s, m])
                        block = ((x - s) % lay.xs * lay.ys + (y ^ m)) * CORES + (c ^ side)
                        blocks.append(block * PARTS + h)
            tile = got.get("tile")
            if step % LANES:
                tile = jnp.zeros(shape, jnp.float32) if tile is None else tile
                for chunk, block in zip(chunks, blocks):
                    dims = (((0,), (0,)), ((), ()))
                    part = lax.dot_general(got["rows"], chunk, dims, preferred_element_type=jnp.float32)
                    tile = lax.dynamic_update_slice(tile, part, (0, block * step))
                got["tile"] = tile
            else:
                got["tile"], got["mark", "tile"] = multiply(tile, got["rows"], chunks, blocks, narrow_at, shape, width)

        row_of(1, 0)
        settle()

        pair(0)
        cross("own", 0)
        own_x(0)
        row_of(0, 0)
        mate("own", 0)
        settle()

        outer("own", 0)
        cross("pair", 0)
        own_x(1)
        row(1)
        mate("own", 1)
        settle()

        outer("pair", 0)
        cross("own", 1)
        near_x(0)
        give(0)
        join_rows(0)
        mate("row", 0)
        lay_row(0, 0)
        settle()

        give_x(0)
        give_more(0)
        pair(1)
        mate("row", 1)
        swap("", 0)
        lay_row(0, 1)
        settle()

        outer("own", 1)
        cross("pair", 1)
        more_x(0)
        back(0)
        swap("y", 0)
        for m in others:
            lay_row(m, 0)
        for m in others:
            lay_row(m, 1)
        settle()

        outer("pair", 1)
        near_x(1)
        give(1)
        swap("x", 0)
        swap("xy", 0)
        product(0, "", "y")
        settle()

        give_x(1)
        give_more(1)
        swap("", 1)
        product(0, "x", "xy")
        settle()

        more_x(1)
        back(1)
        swap("y", 1)
        take("swapped", 1, 0, True)
        product(1, "", "y")
        settle()

        swap("x", 1)
        swap("xy", 1)
        product(1, "x", "xy", sides=(0,))
        settle()

        product(1, "x", "xy", sides=(1,))
        return got["tile"]

    placed = (P(None, AXES), P())
    return jax.shard_map(
        body, mesh=mesh, in_specs=placed, out_specs=P("wide", "narrow"), check_vma=False
    )
```

```python
import jax
import jax.numpy as jnp
from jax import lax
from jax.experimental import pallas as pl
from jax.experimental.pallas import tpu as pltpu
from jax.sharding import PartitionSpec as P

AXES = ("wide", "narrow")
CORES = 2
LANES = 128
PARTS = 2
TURN = 512
VMEM_MIB = 36


class Layout:
    def __init__(self, mesh):
        self.wide, self.narrow = mesh.shape["wide"], mesh.shape["narrow"]
        self.xs = self.wide // self.narrow
        self.zs = self.narrow
        self.ys = self.narrow // CORES
        self.sites = [
            (z, x, y, c)
            for z in range(self.zs)
            for x in range(self.xs)
            for y in range(self.ys)
            for c in range(CORES)
        ]

    def index(self, z, x, y, c):
        return ((z * self.xs + x) * self.ys + y) * CORES + c

    def moves(self, target):
        pairs = []
        for site in self.sites:
            to = target(*site)
            if to is not None:
                pairs.append((self.index(*site), self.index(*to)))
        return pairs


def weigh(panel, row_scale):
    return (panel.astype(jnp.float32) * row_scale).astype(jnp.bfloat16)


def inner(z):
    return (z % 4 == 1) | (z % 4 == 2)


def apart(z, y):
    return (z // CORES) ^ y


def choose(options, index):
    picked = options[0]
    for at in range(1, len(options)):
        picked = jnp.where(index == at, options[at], picked)
    return picked


def to_mate(z, x, y, c):
    return z, x, y, 1 - c


def to_pair(z, x, y, c):
    return z ^ 1, x, y, c


def to_cross(z, x, y, c):
    return (z ^ 3, x, y, c) if inner(z) else None


def to_outer(z, x, y, c):
    return (z ^ 1, x, y, c) if inner(z) else None


def to_far(q):
    return lambda z, x, y, c: (z ^ (CORES * q), x, y, c)


def along_y(m):
    return lambda z, x, y, c: (z, x, y ^ m, c)


def along_x(lay, s, who=lambda z, y: True):
    return lambda z, x, y, c: (z, (x + s) % lay.xs, y, c) if who(z, y) else None


def turn(rows, chunks, at, shape):
    depth, step = chunks[0].shape

    def kernel(*refs):
        chunk_refs, out_ref, token_ref = refs[: len(chunks)], refs[-2], refs[-1]
        for k, ref in enumerate(chunk_refs):
            out_ref[k * step : (k + 1) * step, :] = ref[...].T
        token_ref[...] = jnp.zeros_like(token_ref)

    operands = list(chunks)
    in_specs = [pl.BlockSpec((TURN, step), lambda i: (i, 0)) for _ in chunks]
    aliases = {}
    if rows is not None:
        operands.append(rows)
        in_specs.append(pl.BlockSpec(memory_space=pl.ANY))
        aliases = {len(operands) - 1: 0}
    return pl.pallas_call(
        kernel,
        grid=(depth // TURN,),
        in_specs=in_specs,
        out_specs=[
            pl.BlockSpec((step * len(chunks), TURN), lambda i: (at, i)),
            pl.BlockSpec((8, LANES), lambda i: (0, 0)),
        ],
        out_shape=[
            jax.ShapeDtypeStruct(shape, jnp.bfloat16),
            jax.ShapeDtypeStruct((8, LANES), jnp.float32),
        ],
        input_output_aliases=aliases,
        compiler_params=pltpu.CompilerParams(vmem_limit_bytes=VMEM_MIB * 2**20),
        cost_estimate=pl.CostEstimate(
            flops=0, bytes_accessed=4 * depth * step * len(chunks), transcendentals=0
        ),
    )(*operands)


def multiply(tile, rows, chunks, blocks, place, shape, band):
    high, depth = rows.shape
    step, count = chunks[0].shape[1], len(chunks)
    bands = high // band

    def kernel(blocks_ref, place_ref, rows_ref, *refs):
        chunk_refs = refs[:count]
        tile_ref, token_ref, result, sems = refs[-4:]
        i = pl.program_id(0)

        def copies(i):
            at = pl.multiple_of((i ^ place_ref[0]) * band, band)
            return [
                pltpu.make_async_copy(
                    result.at[i % 2, :, k * step : (k + 1) * step],
                    tile_ref.at[pl.ds(at, band), pl.ds(pl.multiple_of(blocks_ref[k] * step, step), step)],
                    sems.at[i % 2, k],
                )
                for k in range(count)
            ]

        @pl.when(i >= 2)
        def _():
            for copy in copies(i - 2):
                copy.wait()

        right = jnp.concatenate([ref[...] for ref in chunk_refs], axis=1)
        result[i % 2] = jnp.dot(rows_ref[...], right, preferred_element_type=jnp.float32)
        for copy in copies(i):
            copy.start()

        @pl.when(i == bands - 1)
        def _():
            token_ref[...] = jnp.zeros_like(token_ref)
            for last in range(max(bands - 2, 0), bands):
                for copy in copies(last):
                    copy.wait()

    operands = [rows, *chunks]
    in_specs = [pl.BlockSpec((band, depth), lambda i, b, p: (i, 0))]
    in_specs += [pl.BlockSpec((depth, step), lambda i, b, p: (0, 0)) for _ in chunks]
    aliases = {}
    if tile is not None:
        operands.append(tile)
        in_specs.append(pl.BlockSpec(memory_space=pl.ANY))
        aliases = {len(operands) + 1: 0}
    return pl.pallas_call(
        kernel,
        grid_spec=pltpu.PrefetchScalarGridSpec(
            num_scalar_prefetch=2,
            grid=(bands,),
            in_specs=in_specs,
            out_specs=[
                pl.BlockSpec(memory_space=pl.ANY),
                pl.BlockSpec((8, LANES), lambda i, b, p: (0, 0)),
            ],
            scratch_shapes=[
                pltpu.VMEM((2, band, step * count), jnp.float32),
                pltpu.SemaphoreType.DMA((2, count)),
            ],
        ),
        out_shape=[
            jax.ShapeDtypeStruct(shape, jnp.float32),
            jax.ShapeDtypeStruct((8, LANES), jnp.float32),
        ],
        input_output_aliases=aliases,
        compiler_params=pltpu.CompilerParams(vmem_limit_bytes=VMEM_MIB * 2**20),
        cost_estimate=pl.CostEstimate(
            flops=2 * high * depth * step * count,
            bytes_accessed=2 * high * depth + (2 * depth + 4 * high) * step * count,
            transcendentals=0,
        ),
    )(jnp.stack(blocks), place[None], *operands)


def solution(mesh):
    lay = Layout(mesh)

    def body(jacobian, variance):
        depth, width = jacobian.shape
        step = width // PARTS
        shape = (lay.narrow * width, lay.xs * lay.narrow * width)
        wide_at, narrow_at = lax.axis_index("wide"), lax.axis_index("narrow")
        z, x = wide_at // lay.xs, wide_at % lay.xs
        y, c = narrow_at // CORES, narrow_at % CORES
        is_inner, off = inner(z), apart(z, y)
        home, beside = off == 0, off == 1
        halves, others, shifts = range(2, lay.zs // CORES), range(1, lay.ys), range(1, lay.xs)
        first_kept = ((z % CORES) ^ (is_inner & beside)) == c

        row_scale = lax.rsqrt(variance)[:, None]
        got = {}
        for h in range(PARTS):
            got["own", h] = weigh(jacobian[:, h * step : (h + 1) * step], row_scale)
        running = []

        def across(kind, h):
            return jnp.where(is_inner, got[kind + "_cross", h], got[kind + "_outer", h])

        def first(h, q):
            options = [got["own", h], across("own", h)] + [got["far_own", h, n] for n in halves]
            return choose(options, q)

        def second(h, q):
            options = [got["pair", h], across("pair", h)] + [got["far_pair", h, n] for n in halves]
            return choose(options, q)

        def send(name, value, target):
            running.append((name, lax.ppermute(value, AXES, lay.moves(target))))

        def settle(*under_way):
            got.update(r for r in running if r[0][:2] not in under_way)
            running[:] = [r for r in running if r[0][:2] in under_way]
            got.update(zip(got, lax.optimization_barrier(tuple(got.values()))))

        def take(kind, h, s, many):
            mine = [r for r in running if r[0][:3] == (kind, h, s) and (r[0][3] > 0) == many]
            got.update(mine)
            running[:] = [r for r in running if r[0] not in [n for n, _ in mine]]


        def pair(h):
            send(("pair", h), got["own", h], to_pair)

        def cross(kind, h):
            send((kind + "_cross", h), got[kind, h], to_cross)
            for n in halves:
                send(("far_" + kind, h, n), got[kind, h], to_far(n))

        def outer(kind, h):
            send((kind + "_outer", h), got[kind + "_cross", h], to_outer)


        def row(h):
            for m in others:
                send(("row", h, m), got["own", h], along_y(m))

        def row_of(core, h):
            for m in others:
                who = lambda z, x, y, c, m=m: (z, x, y ^ m, c) if c == core else None
                send(("row_of", h, m, core), got["own", h], who)

        def join_rows(h):
            for m in others:
                got["row", h, m] = jnp.where(c == 0, got["row_of", h, m, 0], got["row_of", h, m, 1])

        def give(h):
            for m in others:
                value = jnp.where(off == m, got["pair", h], first(h, off ^ m))
                send(("give", h, m), value, along_y(m))

        def give_more(h):
            for m in others:
                value = jnp.where(off == m, got["own_x", h, 1], second(h, off ^ m))
                send(("give_more", h, m), value, along_y(m))

        def own_x(h):
            for s in shifts:
                send(("own_x", h, s), got["own", h], along_x(lay, s))

        def near_x(h):
            value = jnp.where(home, got["pair", h], first(h, off))
            for s in shifts:
                send(("near_x", h, s), value, along_x(lay, s))

        def more_x(h):
            for m in others:
                value = jnp.where(home, got["give", h, m], second(h, off))
                for s in shifts:
                    who = lambda z, y, m=m: m == 1 or apart(z, y) == 0
                    send(("more_x", h, s, m), value, along_x(lay, s, who))
                    rest = lambda z, y, m=m: apart(z, y) > 1 or (apart(z, y) == 1 and m != 1)
                    if lay.ys > 2:
                        send(("rest_x", h, s, m), got["give_more", h, m], along_x(lay, s, rest))

        def give_x(h):
            for m in others:
                value = jnp.where(home, second(h, 1), got["give", h, m])
                for s in shifts:
                    who = lambda z, y, m=m: m == 1 or apart(z, y) != 0
                    send(("give_x", h, s, m), value, along_x(lay, s, who))

        def back(h):
            for s in shifts:
                send(("back", h, s), got["give_x", h, s, 1], along_y(1))


        def mate(kind, h):
            for name in [n for n in got if n[0] == kind and n[1] == h]:
                send((kind + "_mate", *name[1:]), got[name], to_mate)

        def places(kind):
            return [(s, m) for s in (shifts if "x" in kind else (0,)) for m in (others if "y" in kind else (0,))]

        def both(h, s, m):
            if s == 0 and m == 0:
                return first(h, off), second(h, off)
            if s == 0:
                return (
                    jnp.where(home, got["row", h, m], got["give", h, m]),
                    jnp.where(home, got["give", h, m], got["give_more", h, m]),
                )
            if m == 0:
                return (
                    jnp.where(home, got["own_x", h, s], got["near_x", h, s]),
                    jnp.where(home, got["near_x", h, s], got["more_x", h, s, 1]),
                )
            last = got.get(("rest_x", h, s, m), got["back", h, s])
            if m == 1 and lay.ys > 2:
                last = jnp.where(beside, got["back", h, s], last)
            return (
                jnp.where(home, got["give_more", h, m], got["give_x", h, s, m]),
                jnp.where(home, got["more_x", h, s, m], last),
            )

        def swap(kind, h):
            for s, m in places(kind):
                one, two = both(h, s, m)
                got["kept", h, s, m] = jnp.where(first_kept, one, two)
                send(("swapped", h, s, m), jnp.where(first_kept, two, one), to_mate)


        def lay_row(m, side):
            kind = ("row" if m else "own") + ("_mate" if side else "")
            chunks = [got[(kind, h, m) if m else (kind, h)] for h in range(PARTS)]
            band = m * CORES + side
            if step % LANES:
                rows = got.get("rows")
                rows = jnp.zeros((depth, shape[0]), jnp.bfloat16) if rows is None else rows
                value = jnp.concatenate(chunks, axis=1)
                got["rows"] = lax.dynamic_update_slice(rows, value, (0, (narrow_at ^ band) * width))
            else:
                got["rows"], got["mark", "row", band] = turn(got.get("rows"), chunks, band, (shape[0], depth))

        def product(h, *kinds, sides=(0, 1)):
            chunks, blocks = [], []
            for kind in kinds:
                for s, m in places(kind):
                    for side in sides:
                        chunks.append(got["swapped" if side else "kept", h, s, m])
                        block = ((x - s) % lay.xs * lay.ys + (y ^ m)) * CORES + (c ^ side)
                        blocks.append(block * PARTS + h)
            tile = got.get("tile")
            if step % LANES:
                tile = jnp.zeros(shape, jnp.float32) if tile is None else tile
                for chunk, block in zip(chunks, blocks):
                    dims = (((0,), (0,)), ((), ()))
                    part = lax.dot_general(got["rows"], chunk, dims, preferred_element_type=jnp.float32)
                    tile = lax.dynamic_update_slice(tile, part, (0, block * step))
                got["tile"] = tile
            else:
                got["tile"], got["mark", "tile"] = multiply(tile, got["rows"], chunks, blocks, narrow_at, shape, width)

        row_of(1, 0)
        settle()

        pair(0)
        cross("own", 0)
        own_x(0)
        row_of(0, 0)
        mate("own", 0)
        settle()

        outer("own", 0)
        cross("pair", 0)
        own_x(1)
        row(1)
        mate("own", 1)
        settle()

        outer("pair", 0)
        cross("own", 1)
        near_x(0)
        give(0)
        join_rows(0)
        mate("row", 0)
        lay_row(0, 0)
        settle()

        give_x(0)
        give_more(0)
        pair(1)
        mate("row", 1)
        swap("", 0)
        lay_row(0, 1)
        settle()

        outer("own", 1)
        cross("pair", 1)
        more_x(0)
        back(0)
        swap("y", 0)
        for m in others:
            lay_row(m, 0)
        for m in others:
            lay_row(m, 1)
        settle()

        outer("pair", 1)
        near_x(1)
        give(1)
        swap("x", 0)
        swap("xy", 0)
        product(0, "", "y")
        settle()

        give_x(1)
        give_more(1)
        swap("", 1)
        product(0, "x", "xy")
        settle()

        more_x(1)
        back(1)
        swap("y", 1)
        take("swapped", 1, 0, True)
        product(1, "", "y")
        settle()

        swap("x", 1)
        swap("xy", 1)
        product(1, "x", "xy", sides=(0,))
        settle()

        product(1, "x", "xy", sides=(1,))
        return got["tile"]

    placed = (P(None, AXES), P())
    return jax.shard_map(
        body, mesh=mesh, in_specs=placed, out_specs=P("wide", "narrow"), check_vma=False
    )
```
